32 devices in a mesh: rep: 2 (over y), seq: 4 (over z), head: 2 (over x), sub: 2 (over core).
Axes of the slice: x: 2, y: 2, z: 4, core: 2. Of those that a mesh axis runs over, the one named last changes fastest.
Arguments:
- conv_inputs: bfloat16 [2048, 3, 4096], P(('rep', 'seq'), None, ('head', 'sub')), parts along dimension 0, may hold values from -6 to 6
- conv_weight: float32 [4, 3, 4096], P(None, None, ('head', 'sub')), may hold values from -3 to 3
- gate_logs: bfloat16 [2048, 4096], P(('rep', 'seq'), ('head', 'sub')), parts along dimension 0, may hold values from -1 to 0, as said below
- beta_rates: float32 [32, 2048], P(('head', 'sub'), ('rep', 'seq')), parts along dimension 1, may hold values from 0.02 to 0.95
- state_resets: int32 [32], P(('rep', 'seq')), parts along dimension 0, may hold values from 0 to 1
- out_grad: bfloat16 [2048, 4096], P(('rep', 'seq'), ('head', 'sub')), parts along dimension 0, may hold values from -6 to 6
Outputs:
- input_grad: bfloat16 [2048, 3, 4096], P(('rep', 'seq'), None, ('head', 'sub')), parts along dimension 0
- gate_grad: bfloat16 [2048, 4096], P(('rep', 'seq'), ('head', 'sub')), parts along dimension 0
- rate_grad: float32 [32, 2048], P(('head', 'sub'), ('rep', 'seq')), parts along dimension 1
- conv_grad: float32 [8, 3, 4096], P('rep', None, ('head', 'sub')), parts along dimension 0
The draws below stay inside these ranges and needn't reach their ends.
There are 2 independent parts, one for each index of `rep`. The reference program is written for one: setup_inputs(seed, part) draws one part's arguments, and reference() takes and returns one part's arrays. A program takes and returns all parts, laid end to end along the dimension named above; an argument that names none is the same for every part. Nothing has to cross between parts.
Inputs may be any that keep to these rules, and one draw needn't show every extreme that they name: gate_logs are log decay factors.
All inputs are finite; a program needn't handle non-finite values.
Results may differ from the reference program's by a relative error of at most 0.0004.
Values may be sent and summed in bfloat16 or wider, within the bound.
A program may use at most 128 MiB of HBM per device.

```python
import math
import jax
import jax.numpy as jnp
from jax import lax

HEADS = 32
DK = 128
KW = 4
TRACE_TOKENS = 1024
NCHUNKS = 16


def slow_heads_of(key):
    slow_share = 5
    return jax.random.randint(jax.random.fold_in(key, 101), (HEADS, 1), 0, 10) < slow_share


def draw_gate_logs(key, part):
    sequence_portions = jax.random.split(key, 6)
    slow_heads = slow_heads_of(key)
    slow_rates = jax.random.uniform(sequence_portions[1], (HEADS, DK), minval=0.03, maxval=0.15) * (2.3 / TRACE_TOKENS)
    fast_rates = jnp.exp(jax.random.uniform(sequence_portions[2], (HEADS, DK), minval=math.log(0.03), maxval=math.log(0.08)))
    forget_strengths = jnp.where(slow_heads, slow_rates, fast_rates)
    jaggedness_level = jax.random.uniform(sequence_portions[3], (TRACE_TOKENS, HEADS, DK), minval=0.5, maxval=2.0)
    spike_positions = jax.random.randint(sequence_portions[4], (2,), 0, TRACE_TOKENS)
    spike_events = jnp.any(jnp.arange(TRACE_TOKENS)[:, None] == spike_positions[None, :], axis=1)
    spike_magnitude = jax.random.uniform(sequence_portions[5], (TRACE_TOKENS, 1, 1), minval=math.log(0.5), maxval=math.log(0.8))
    logarithm_decay = -forget_strengths[None] * jaggedness_level + jnp.where(spike_events[:, None, None], spike_magnitude, 0.0)
    return logarithm_decay.reshape(TRACE_TOKENS, HEADS * DK).astype(jnp.bfloat16)


def draw_beta_rates(key, part):
    slow_heads = slow_heads_of(key)
    sequence_portions = jax.random.split(jax.random.fold_in(key, 7), 2)
    low_rates = jax.random.uniform(sequence_portions[0], (HEADS, TRACE_TOKENS), minval=0.02, maxval=0.06)
    high_rates = jax.random.uniform(sequence_portions[1], (HEADS, TRACE_TOKENS), minval=0.05, maxval=0.95)
    return jnp.where(slow_heads, low_rates, high_rates).astype(jnp.float32)


def draw_state_resets(key, part):
    reset_keys = jax.random.split(jax.random.fold_in(key, 313), 2)
    chosen_blocks = jax.random.randint(reset_keys[0], (2,), 1, NCHUNKS)
    placed = jnp.any(jnp.arange(NCHUNKS)[:, None] == chosen_blocks[None, :], axis=1)
    scattered = jax.random.randint(reset_keys[1], (NCHUNKS,), 0, 64) == 0
    return jnp.logical_or(placed, scattered).astype(jnp.int32)


def block_scale(key, shape, pieces, least, high):
    def one(axis_at, shards_of):
        heights = jax.random.uniform(jax.random.fold_in(jax.random.fold_in(key, 6), axis_at), (shards_of,), jnp.float32, least / len(pieces), high / len(pieces))
        return jnp.repeat(jnp.exp(heights), shape[axis_at] // shards_of).reshape((-1,) + (1,) * (len(shape) - axis_at - 1))

    factor_of = one(*pieces[0])
    for cut in pieces[1:]:
        factor_of = factor_of * one(*cut)
    return factor_of


def centred(own_key, shape, deviation, most, cuts=(), kind=jnp.bfloat16):
    values = jax.random.normal(own_key, shape, jnp.float32) * deviation
    if len(cuts) > 0:
        values = block_scale(own_key, shape, cuts, -0.22, 0.18) * values
    return jnp.clip(values, min=-most, max=most).astype(kind)


def setup_inputs(seed: int = 0, part: int = 0) -> dict:
    splits = jax.random.split(jax.random.key(seed), 7)
    own_keys = jax.random.split(jax.random.fold_in(splits[6], part), 7)
    return {
        "conv_inputs": centred(own_keys[0], (TRACE_TOKENS, 3, HEADS * DK), 1.0, 6.0, ((0, 4), (2, 4))),
        "conv_weight": centred(splits[1], (KW, 3, HEADS * DK), KW ** -0.5, 3.0, ((2, 4),), jnp.float32),
        "gate_logs": draw_gate_logs(jax.random.fold_in(jax.random.fold_in(splits[6], part), 71), part),
        "beta_rates": draw_beta_rates(jax.random.fold_in(jax.random.fold_in(splits[6], part), 71), part),
        "state_resets": draw_state_resets(jax.random.fold_in(jax.random.fold_in(splits[6], part), 71), part),
        "out_grad": centred(own_keys[5], (TRACE_TOKENS, HEADS * DK), 1.0, 6.0, ((0, 4), (1, 4))),
    }


HIGH_PRECISION = lax.Precision.HIGHEST

def features(extended, weight):
    row_count = extended.shape[0] - (KW - 1)
    mixture = weight[0][None] * extended[0:row_count]
    for offset in range(1, KW):
        mixture = mixture + weight[offset][None] * extended[offset:offset + row_count]
    activated = jax.nn.silu(mixture)
    head_count = activated.shape[2] // DK
    queries = activated[:, 0].reshape(row_count, head_count, DK)
    key_rows = activated[:, 1].reshape(row_count, head_count, DK)
    values = activated[:, 2].reshape(row_count, head_count, DK)
    queries = queries / jnp.sqrt(lax.optimization_barrier(jnp.sum(queries * queries, axis=2, keepdims=True)) + 1e-06) * DK ** (-0.5)
    key_rows = key_rows / jnp.sqrt(lax.optimization_barrier(jnp.sum(key_rows * key_rows, axis=2, keepdims=True)) + 1e-06)
    return (queries, key_rows, values)

def group_step(state_now, inputs):
    queries, key_rows, values, gate_rows, betas, keep_flag = inputs
    initial_state = state_now * keep_flag
    decays = jnp.cumsum(gate_rows, axis=1)
    key_plus = key_rows * jnp.exp(decays)
    key_minus = key_rows * jnp.exp(-decays)
    query_boosted = queries * jnp.exp(decays)
    length = key_rows.shape[1]
    later_mask = (jnp.arange(length)[:, None] > jnp.arange(length)[None, :]).astype(jnp.float32)
    upto_mask = later_mask + jnp.eye(length, dtype=jnp.float32)
    products = jnp.einsum('hsk,hrk->hsr', key_plus, key_minus, precision=HIGH_PRECISION)
    system = jnp.eye(length, dtype=jnp.float32)[None] + products * betas[:, :, None] * later_mask[None]
    right_side = jnp.concatenate([betas[:, :, None] * values, betas[:, :, None] * key_plus], axis=2)
    triangular_solution = jax.scipy.linalg.solve_triangular(system, right_side, lower=True, unit_diagonal=True)
    kernel_width = values.shape[2]
    state_update = triangular_solution[:, :, :kernel_width] - jnp.einsum('uaf,ufg->uag', triangular_solution[:, :, kernel_width:], initial_state, precision=HIGH_PRECISION)
    query_key_scores = jnp.einsum('htk,hsk->hts', query_boosted, key_minus, precision=HIGH_PRECISION) * upto_mask[None]
    layer_output = jnp.einsum('srp,spm->srm', query_boosted, initial_state, precision=HIGH_PRECISION) + jnp.einsum('zlp,zpo->zlo', query_key_scores, state_update, precision=HIGH_PRECISION)
    final_decay_factor = decays[:, -1:, :]
    key_final_scaled = key_rows * jnp.exp(final_decay_factor - decays)
    upcoming_state = jnp.exp(final_decay_factor[:, 0, :])[:, :, None] * initial_state + jnp.einsum('tiz,tib->tzb', key_final_scaled, state_update, precision=HIGH_PRECISION)
    return (upcoming_state, layer_output)

def to_blocks(array, group_count):
    return array.reshape(group_count, -1, array.shape[1], array.shape[2]).transpose(0, 2, 1, 3)

def run_groups(state_first, queries, key_rows, values, gate_rows, betas, keep_flags):
    group_count = keep_flags.shape[0]
    beta_blocks = betas.reshape(betas.shape[0], group_count, -1).transpose(1, 0, 2)
    final, outputs = lax.scan(jax.checkpoint(group_step), state_first, (to_blocks(queries, group_count), to_blocks(key_rows, group_count), to_blocks(values, group_count), to_blocks(gate_rows, group_count), beta_blocks, keep_flags))
    outputs = outputs.transpose(0, 2, 1, 3).reshape(queries.shape)
    return (outputs, final)

def reference(conv_inputs, conv_weight, gate_logs, beta_rates, state_resets, out_grad):
    margin = KW - 1
    token_count = conv_inputs.shape[0]
    padding = jnp.zeros((margin,) + conv_inputs.shape[1:], jnp.float32)
    extended = jnp.concatenate([padding, conv_inputs.astype(jnp.float32)], axis=0)
    keep_flags = 1.0 - state_resets.astype(jnp.float32)
    head_count = beta_rates.shape[0]

    def whole(extended_rows, weight, gate_rows, betas):
        queries, key_rows, values = features(extended_rows, weight)
        zero_state = jnp.zeros((head_count, DK, DK), jnp.float32)
        outputs, final = run_groups(zero_state, queries, key_rows, values, gate_rows, betas, keep_flags)
        return outputs
    gate_rows = gate_logs.astype(jnp.float32).reshape(token_count, head_count, DK)
    outputs, backward = jax.vjp(whole, extended, conv_weight, gate_rows, beta_rates)
    d_extended, d_weight, d_gates, d_betas = backward(out_grad.astype(jnp.float32).reshape(token_count, head_count, DK))
    return (d_extended[margin:].astype(jnp.bfloat16), d_gates.reshape(token_count, head_count * DK).astype(jnp.bfloat16), d_betas, d_weight)
```

```python
import jax
import jax.numpy as jnp
from jax import lax
from jax.sharding import PartitionSpec as P

DK = 128
KW = 4


HIGH_PRECISION = lax.Precision.HIGHEST


def from_behind(array, axis, by):
    count = lax.axis_size(axis)
    pairs = [(i, i + by) for i in range(count) if 0 <= i + by < count]
    return lax.ppermute(array, axis, pairs)


def carried_in(part, axis, combine, identity, reverse):
    count = lax.axis_size(axis)
    place = lax.axis_index(axis)
    ahead = count - 1 - place if reverse else place
    gathered = jax.tree.map(lambda a: lax.all_gather(a, axis), part)
    state = jax.tree.map(lambda a, e: jnp.zeros_like(a) + jnp.asarray(e, a.dtype), part, identity)

    def one(turn, state):
        source = count - 1 - turn if reverse else turn
        return combine(
            state, jax.tree.map(lambda a: lax.dynamic_index_in_dim(a, source, 0, False), gathered)
        )

    return lax.fori_loop(0, ahead, one, state)


def features(extended, weight):
    row_count = extended.shape[0] - (KW - 1)
    mixture = weight[0][None] * extended[0:row_count]
    for offset in range(1, KW):
        mixture = mixture + weight[offset][None] * extended[offset : offset + row_count]
    activated = jax.nn.silu(mixture)
    head_count = activated.shape[2] // DK
    queries = activated[:, 0].reshape(row_count, head_count, DK)
    key_rows = activated[:, 1].reshape(row_count, head_count, DK)
    values = activated[:, 2].reshape(row_count, head_count, DK)
    queries = (
        queries / jnp.sqrt(jnp.sum(queries * queries, axis=2, keepdims=True) + 1e-06) * DK ** (-0.5)
    )
    key_rows = key_rows / jnp.sqrt(jnp.sum(key_rows * key_rows, axis=2, keepdims=True) + 1e-06)
    return (queries, key_rows, values)


def running_sum(rows):
    length = rows.shape[1]
    upto = (jnp.arange(length)[:, None] >= jnp.arange(length)[None, :]).astype(jnp.float32)
    return jnp.einsum("ts,hsk->htk", upto, rows, precision=HIGH_PRECISION)


def group_step(state_now, inputs):
    queries, key_rows, values, gate_rows, betas, keep_flag = inputs
    initial_state = state_now * keep_flag
    decays = running_sum(gate_rows)
    key_plus = key_rows * jnp.exp(decays)
    key_minus = key_rows * jnp.exp(-decays)
    query_boosted = queries * jnp.exp(decays)
    length = key_rows.shape[1]
    later_mask = (jnp.arange(length)[:, None] > jnp.arange(length)[None, :]).astype(jnp.float32)
    upto_mask = later_mask + jnp.eye(length, dtype=jnp.float32)
    products = jnp.einsum("hsk,hrk->hsr", key_plus, key_minus, precision=HIGH_PRECISION)
    system = (
        jnp.eye(length, dtype=jnp.float32)[None] + products * betas[:, :, None] * later_mask[None]
    )
    right_side = jnp.concatenate([betas[:, :, None] * values, betas[:, :, None] * key_plus], axis=2)
    triangular_solution = jax.scipy.linalg.solve_triangular(
        system, right_side, lower=True, unit_diagonal=True
    )
    kernel_width = values.shape[2]
    state_update = triangular_solution[:, :, :kernel_width] - jnp.einsum(
        "uaf,ufg->uag",
        triangular_solution[:, :, kernel_width:],
        initial_state,
        precision=HIGH_PRECISION,
    )
    query_key_scores = (
        jnp.einsum("htk,hsk->hts", query_boosted, key_minus, precision=HIGH_PRECISION)
        * upto_mask[None]
    )
    layer_output = jnp.einsum(
        "srp,spm->srm", query_boosted, initial_state, precision=HIGH_PRECISION
    ) + jnp.einsum("zlp,zpo->zlo", query_key_scores, state_update, precision=HIGH_PRECISION)
    final_decay_factor = decays[:, -1:, :]
    key_final_scaled = key_rows * jnp.exp(final_decay_factor - decays)
    upcoming_state = jnp.exp(final_decay_factor[:, 0, :])[:, :, None] * initial_state + jnp.einsum(
        "tiz,tib->tzb", key_final_scaled, state_update, precision=HIGH_PRECISION
    )
    return (upcoming_state, layer_output)


def block_parts(key_rows, values, gate_rows, betas):
    decays = running_sum(gate_rows)
    key_plus = key_rows * jnp.exp(decays)
    key_minus = key_rows * jnp.exp(-decays)
    length = key_rows.shape[1]
    later_mask = (jnp.arange(length)[:, None] > jnp.arange(length)[None, :]).astype(jnp.float32)
    products = jnp.einsum("hsk,hrk->hsr", key_plus, key_minus, precision=HIGH_PRECISION)
    system = (
        jnp.eye(length, dtype=jnp.float32)[None] + products * betas[:, :, None] * later_mask[None]
    )
    right_side = jnp.concatenate([betas[:, :, None] * values, betas[:, :, None] * key_plus], axis=2)
    triangular_solution = jax.scipy.linalg.solve_triangular(
        system, right_side, lower=True, unit_diagonal=True
    )
    final_decay_factor = decays[:, -1:, :]
    key_final_scaled = key_rows * jnp.exp(final_decay_factor - decays)
    return (decays, key_minus, triangular_solution, key_final_scaled, final_decay_factor)


def group_map(carried, inputs):
    key_rows, values, gate_rows, betas, keep_flag = inputs
    decays, key_minus, triangular_solution, key_final_scaled, final_decay_factor = block_parts(
        key_rows, values, gate_rows, betas
    )
    kernel_width = values.shape[2]
    diagonal = (
        jnp.exp(final_decay_factor[:, 0, :])[:, :, None] * jnp.eye(DK, dtype=jnp.float32)[None]
    )
    through = (
        diagonal
        - jnp.einsum(
            "hck,hcj->hkj",
            key_final_scaled,
            triangular_solution[:, :, kernel_width:],
            precision=HIGH_PRECISION,
        )
    ) * keep_flag
    shift_contribution = jnp.einsum(
        "tiz,tib->tzb",
        key_final_scaled,
        triangular_solution[:, :, :kernel_width],
        precision=HIGH_PRECISION,
    )
    return (
        (compose_mat(through, carried[0]), compose_mat(through, carried[1]) + shift_contribution),
        None,
    )


def start_grad_step(following_gradient, inputs):
    queries, key_rows, values, gate_rows, betas, keep_flag, output_gradient = inputs
    decays, key_minus, triangular_solution, key_final_scaled, final_decay_factor = block_parts(
        key_rows, values, gate_rows, betas
    )
    kernel_width = values.shape[2]
    query_boosted = queries * jnp.exp(decays)
    length = key_rows.shape[1]
    upto_mask = (jnp.arange(length)[:, None] >= jnp.arange(length)[None, :]).astype(jnp.float32)
    query_key_scores = (
        jnp.einsum("htk,hsk->hts", query_boosted, key_minus, precision=HIGH_PRECISION)
        * upto_mask[None]
    )
    update_gradient = jnp.einsum(
        "hts,htv->hsv", query_key_scores, output_gradient, precision=HIGH_PRECISION
    ) + jnp.einsum("uaf,ufg->uag", key_final_scaled, following_gradient, precision=HIGH_PRECISION)
    initial_state_gradient = jnp.einsum(
        "ndi,ndx->nix", query_boosted, output_gradient, precision=HIGH_PRECISION
    )
    initial_state_gradient = (
        initial_state_gradient
        + jnp.exp(final_decay_factor[:, 0, :])[:, :, None] * following_gradient
    )
    initial_state_gradient = initial_state_gradient - jnp.einsum(
        "tiz,tib->tzb",
        triangular_solution[:, :, kernel_width:],
        update_gradient,
        precision=HIGH_PRECISION,
    )
    return (initial_state_gradient * keep_flag, None)


def compose_mat(left_mat, right_mat):
    return jnp.einsum("hij,hjk->hik", left_mat, right_mat, precision=HIGH_PRECISION)


def combine(earlier, later_map):
    return (
        compose_mat(later_map[0], earlier[0]),
        compose_mat(later_map[0], earlier[1]) + later_map[1],
    )


def to_blocks(array, group_count):
    return array.reshape(group_count, -1, array.shape[1], array.shape[2]).transpose(0, 2, 1, 3)


def run_groups(state_first, queries, key_rows, values, gate_rows, betas, keep_flags):
    group_count = keep_flags.shape[0]
    beta_blocks = betas.reshape(betas.shape[0], group_count, -1).transpose(1, 0, 2)
    final, outputs = lax.scan(
        jax.checkpoint(group_step),
        state_first,
        (
            to_blocks(queries, group_count),
            to_blocks(key_rows, group_count),
            to_blocks(values, group_count),
            to_blocks(gate_rows, group_count),
            beta_blocks,
            keep_flags,
        ),
    )
    outputs = outputs.transpose(0, 2, 1, 3).reshape(queries.shape)
    return (outputs, final)


def on_device(conv_inputs, conv_weight, gate_logs, beta_rates, state_resets, out_grad):
    token_count = conv_inputs.shape[0]
    margin = KW - 1
    rim_rows = from_behind(conv_inputs[token_count - margin :], "seq", 1)
    extended = jnp.concatenate([rim_rows, conv_inputs], axis=0).astype(jnp.float32)
    (queries, key_rows, values), feature_back = jax.vjp(features, extended, conv_weight)
    head_count = queries.shape[1]
    gate_rows = gate_logs.astype(jnp.float32).reshape(token_count, head_count, DK)
    keep_flags = 1.0 - state_resets.astype(jnp.float32)
    group_count = keep_flags.shape[0]
    identity = jnp.broadcast_to(jnp.eye(DK, dtype=jnp.float32)[None], (head_count, DK, DK))
    zero_state = jnp.zeros((head_count, DK, DK), jnp.float32)
    beta_blocks = beta_rates.reshape(head_count, group_count, -1).transpose(1, 0, 2)
    query_blocks = to_blocks(queries, group_count)
    key_blocks = to_blocks(key_rows, group_count)
    value_blocks = to_blocks(values, group_count)
    gate_blocks = to_blocks(gate_rows, group_count)
    (through, offset_sum), unused = lax.scan(
        group_map,
        (identity, zero_state),
        (key_blocks, value_blocks, gate_blocks, beta_blocks, keep_flags),
    )
    carried = carried_in((through, offset_sum), "seq", combine, (identity, zero_state), False)
    state_in = carried[1]

    def shard_pass(state_first, query_part, key_part, value_part, gate_part, beta_part):
        return run_groups(
            state_first, query_part, key_part, value_part, gate_part, beta_part, keep_flags
        )

    (outputs, state_out), shard_back = jax.vjp(
        shard_pass, state_in, queries, key_rows, values, gate_rows, beta_rates
    )
    d_rows = out_grad.astype(jnp.float32).reshape(token_count, head_count, DK)
    own_term, unused_rows = lax.scan(
        start_grad_step,
        zero_state,
        (
            query_blocks,
            key_blocks,
            value_blocks,
            gate_blocks,
            beta_blocks,
            keep_flags,
            to_blocks(d_rows, group_count),
        ),
        reverse=True,
    )
    flipped = jnp.swapaxes(through, 1, 2)
    carried_back = carried_in((flipped, own_term), "seq", combine, (identity, zero_state), True)
    state_grad = carried_back[1]
    full_grads = shard_back((d_rows, state_grad))
    d_queries, d_keys, d_values, d_gates, d_betas = (
        full_grads[1],
        full_grads[2],
        full_grads[3],
        full_grads[4],
        full_grads[5],
    )
    d_extended, d_weight = feature_back((d_queries, d_keys, d_values))
    spill_rows = from_behind(d_extended[:margin], "seq", -1)
    d_inputs = d_extended[margin:]
    d_inputs = d_inputs.at[token_count - margin :].add(spill_rows)
    conv_total = lax.psum(d_weight, "seq")
    return (
        d_inputs.astype(jnp.bfloat16),
        d_gates.reshape(token_count, head_count * DK).astype(jnp.bfloat16),
        d_betas,
        conv_total,
    )


def solution(mesh):
    in_specs = (
        P(("rep", "seq"), None, ("head", "sub")),
        P(None, None, ("head", "sub")),
        P(("rep", "seq"), ("head", "sub")),
        P(("head", "sub"), ("rep", "seq")),
        P(("rep", "seq")),
        P(("rep", "seq"), ("head", "sub")),
    )
    out_specs = (
        P(("rep", "seq"), None, ("head", "sub")),
        P(("rep", "seq"), ("head", "sub")),
        P(("head", "sub"), ("rep", "seq")),
        P("rep", None, ("head", "sub")),
    )
    return jax.shard_map(
        on_device, mesh=mesh, in_specs=in_specs, out_specs=out_specs, check_vma=False
    )
```

```python
import jax
import jax.numpy as jnp
from jax import lax
from jax.experimental import pallas as pl
from jax.experimental.pallas import tpu as pltpu
from jax.sharding import PartitionSpec as P

DK = 128
KW = 4
BLOCK = 64
SCALE = DK ** (-0.5)
F32 = jnp.float32
BF16 = jnp.bfloat16


def shifted(array, axis, by):
    count = lax.axis_size(axis)
    pairs = [(i, i + by) for i in range(count) if 0 <= i + by < count]
    return lax.ppermute(array, axis, pairs)


def split(a):
    high = a.astype(BF16)
    return (high, (a - high.astype(F32)).astype(BF16))


def dot(a, b, ca, cb):
    return lax.dot_general(a, b, (((ca,), (cb,)), ((), ())), preferred_element_type=F32)


def mm(a, b, ca=1, cb=0):
    out = dot(a[0], b[0], ca, cb)
    if len(b) > 1:
        out = out + dot(a[0], b[1], ca, cb)
    if len(a) > 1:
        out = out + dot(a[1], b[0], ca, cb)
    return out


def rows_of(a, b):
    return tuple(p[b * BLOCK : (b + 1) * BLOCK] for p in a)


def positions(count):
    r = lax.broadcasted_iota(jnp.int32, (count, count), 0)
    c = lax.broadcasted_iota(jnp.int32, (count, count), 1)
    return r, c, jnp.bitwise_xor(r, c)


def column(row):
    return jnp.transpose(jnp.broadcast_to(row, (DK, row.shape[1])))


def local_terms(x_ref, rim_ref, w_ref, g_ref, upto):
    count = x_ref.shape[1]
    taps, mixed, sigs, acts = [], [], [], []
    for c in range(3):
        ext = jnp.concatenate([rim_ref[c].astype(F32), x_ref[c].astype(F32)], axis=0)
        rolled = [pltpu.roll(ext, KW - 1 - j, 0)[8:] if j < KW - 1 else ext[8:] for j in range(KW)]
        y = w_ref[c, 0:1] * rolled[0]
        for j in range(1, KW):
            y = y + w_ref[c, j : j + 1] * rolled[j]
        sig = 1.0 / (1.0 + jnp.exp(-y))
        taps.append(rolled)
        mixed.append(y)
        sigs.append(sig)
        acts.append(y * sig)
    rq = lax.rsqrt(jnp.sum(acts[0] * acts[0], axis=1, keepdims=True) + 1e-6)
    rk = lax.rsqrt(jnp.sum(acts[1] * acts[1], axis=1, keepdims=True) + 1e-6)
    q = acts[0] * rq * SCALE
    k = acts[1] * rk
    decays = dot(upto, g_ref[...], 1, 0)
    ends = [decays[b * BLOCK + BLOCK - 1 : (b + 1) * BLOCK] for b in range(count // BLOCK)]
    last = jnp.concatenate([jnp.broadcast_to(e, (BLOCK, DK)) for e in ends], axis=0)
    return taps, mixed, sigs, acts, rq, rk, q, k, decays, last, ends


def maps_kernel(
    resets_ref, x_ref, rim_ref, w_ref, g_ref, beta_ref, do_ref,
    x_out, w_out, u_out, pdo_out, mb_out, nb_out, gb_out, m_out, n_out, g_out,
):
    count = x_ref.shape[1]
    blocks = count // BLOCK
    r, c, x = positions(count)
    inside = x < BLOCK
    upto_mask = inside & (r >= c)
    upto = upto_mask.astype(F32).astype(BF16)
    taps, mixed, sigs, acts, rq, rk, q, k, decays, last, ends = local_terms(
        x_ref, rim_ref, w_ref, g_ref, upto
    )
    v = acts[2]
    grow = jnp.exp(decays)
    kp = k * grow
    km = split(k * jnp.exp(-decays))
    qb = split(q * grow)
    kf = split(k * jnp.exp(last - decays))
    beta = column(beta_ref[pl.ds(pl.program_id(0), 1), :])
    wide = jnp.concatenate([beta] * (count // DK), axis=1)
    n = mm(split(kp), km, 1, 1) * wide
    lower = r > c
    inv = jnp.where(r == c, 1.0, 0.0) - jnp.where(lower & (x < 2) & (x >= 1), n, 0.0)
    s = 2
    while s < BLOCK:
        level = split(jnp.where(lower & (x >= s) & (x < 2 * s), n, 0.0))
        inv_s = split(inv)
        inv = inv - mm(split(mm(inv_s, level)), inv_s)
        s *= 2
    x_out[0] = inv
    both = mm(split(inv), split(jnp.concatenate([beta * v, beta * kp], axis=1)))
    u0 = both[:, :DK]
    w = both[:, DK:]
    u_out[...] = u0
    w_out[...] = w
    do = (do_ref[...],)
    p = split(jnp.where(upto_mask, mm(qb, km, 1, 1), 0.0))
    pdo = mm(p, do, 0, 0)
    pdo_out[...] = pdo
    both_s = split(both)
    pdo_s = split(pdo)
    w_s = split(w)
    er = lax.broadcasted_iota(jnp.int32, (DK, DK), 0) == lax.broadcasted_iota(jnp.int32, (DK, DK), 1)
    ms, gs = [], []
    acc = None
    for b in range(blocks):
        keep = 1.0 - resets_ref[b].astype(F32)
        nm = mm(rows_of(kf, b), rows_of(both_s, b), 0, 0)
        m = (jnp.where(er, jnp.exp(ends[b]), 0.0) - nm[:, DK:]) * keep
        nb = nm[:, :DK]
        g = mm(rows_of(qb, b), rows_of(do, b), 0, 0) - mm(rows_of(w_s, b), rows_of(pdo_s, b), 0, 0)
        g = g * keep
        mb_out[0, b] = m
        nb_out[0, b] = nb
        gb_out[0, b] = g
        m_s = split(m)
        ms.append(m_s)
        gs.append(g)
        if acc is None:
            acc = jnp.concatenate([m, nb], axis=1)
        else:
            acc = mm(m_s, split(acc))
            acc = jnp.concatenate([acc[:, :DK], acc[:, DK:] + nb], axis=1)
    m_out[0] = acc[:, :DK]
    n_out[0] = acc[:, DK:]
    grad = gs[-1]
    for b in range(blocks - 2, -1, -1):
        grad = mm(ms[b], split(grad), 0, 0) + gs[b]
    g_out[0] = grad


def grads_kernel(
    resets_ref, x_ref, rim_ref, w_ref, g_ref, beta_ref, do_ref,
    inv_ref, wm_ref, u_ref, pdo_ref, mb_ref, nb_ref, gb_ref, s_ref, ds_ref,
    dx_out, dg_out, db_out, dw_out, edge_out,
):
    count = x_ref.shape[1]
    blocks = count // BLOCK
    r, c, x = positions(count)
    inside = x < BLOCK
    upto_mask = inside & (r >= c)
    upto = upto_mask.astype(F32).astype(BF16)
    taps, mixed, sigs, acts, rq, rk, q, k, decays, last, ends = local_terms(
        x_ref, rim_ref, w_ref, g_ref, upto
    )
    v = acts[2]
    grow = jnp.exp(decays)
    shrink = jnp.exp(-decays)
    tail = jnp.exp(last - decays)
    kp, km, qb, kf = k * grow, k * shrink, q * grow, k * tail
    kp_s, km_s, qb_s, kf_s = split(kp), split(km), split(qb), split(kf)
    beta = column(beta_ref[pl.ds(pl.program_id(0), 1), :])
    do = do_ref[...]

    ms = [split(mb_ref[0, b]) for b in range(blocks)]
    states = []
    now = s_ref[0]
    for b in range(blocks):
        states.append(now * (1.0 - resets_ref[b].astype(F32)))
        if b < blocks - 1:
            now = mm(ms[b], split(now)) + nb_ref[0, b]
    states_s = [split(a) for a in states]
    after = [None] * blocks
    after[-1] = ds_ref[0]
    for b in range(blocks - 1, 0, -1):
        after[b - 1] = mm(ms[b], split(after[b]), 0, 0) + gb_ref[0, b]
    after_s = [split(a) for a in after]

    w_s = split(wm_ref[...])
    u = u_ref[...] - jnp.concatenate([mm(rows_of(w_s, b), states_s[b]) for b in range(blocks)], axis=0)
    u_s = split(u)
    du = pdo_ref[...] + jnp.concatenate([mm(rows_of(kf_s, b), after_s[b]) for b in range(blocks)], axis=0)
    drv = mm(split(inv_ref[0]), split(du), 0, 0)
    drv_s = split(drv)
    do_s = (do,)
    dp_s = split(jnp.where(upto_mask, mm(do_s, u_s, 1, 1), 0.0))
    dt = jnp.where(inside & (r > c), mm(drv_s, u_s, 1, 1), 0.0)
    dt_s = split(-dt)
    dq_state, drw, dkf, extra = [], [], [], []
    ones = (jnp.ones((8, DK), BF16),)
    for b in range(blocks):
        dq_state.append(mm(rows_of(do_s, b), states_s[b], 1, 1))
        drw.append(-mm(rows_of(drv_s, b), states_s[b], 1, 1))
        dkf.append(mm(rows_of(u_s, b), after_s[b], 1, 1))
        extra.append(mm(ones, split(states[b] * after[b]), 1, 1)[0:1] * jnp.exp(ends[b]))
    dqb = jnp.concatenate(dq_state, axis=0) + mm(dp_s, km_s)
    inner = jnp.concatenate(drw, axis=0) + mm(dt_s, km_s)
    dkf = jnp.concatenate(dkf, axis=0)
    dkp = beta * inner
    wide = jnp.concatenate([beta] * (count // DK), axis=1)
    da_s = split(-dt * wide)
    dkm = mm(dp_s, qb_s, 0, 0) + mm(da_s, kp_s, 0, 0)
    dbeta = jnp.sum(drv * v + kp * inner, axis=1, keepdims=True)
    db_out[pl.ds(pl.program_id(0), 1), :] = jnp.transpose(jnp.broadcast_to(dbeta, (count, DK)))[0:1]

    through = dkf * kf
    dd = dkp * kp - dkm * km - through + dqb * qb
    dg = mm((upto,), split(dd), 0, 0)
    whole = []
    for b in range(blocks):
        total = jnp.sum(through[b * BLOCK : (b + 1) * BLOCK], axis=0, keepdims=True) + extra[b]
        whole.append(jnp.broadcast_to(total, (BLOCK, DK)))
    dg_out[...] = (dg + jnp.concatenate(whole, axis=0)).astype(BF16)

    dq = dqb * grow
    dk = dkp * grow + dkm * shrink + dkf * tail
    dv = beta * drv
    da_q = SCALE * rq * dq - acts[0] * (rq * rq) * jnp.sum(q * dq, axis=1, keepdims=True)
    da_k = rk * dk - acts[1] * (rk * rk) * jnp.sum(k * dk, axis=1, keepdims=True)
    zeros = jnp.zeros((8, DK), F32)
    for ch, da in enumerate((da_q, da_k, dv)):
        dy = da * sigs[ch] * (1.0 + mixed[ch] * (1.0 - sigs[ch]))
        ext = jnp.concatenate([zeros, dy], axis=0)
        full = w_ref[ch, KW - 1 : KW] * ext
        for j in range(KW - 1):
            full = full + w_ref[ch, j : j + 1] * pltpu.roll(ext, count + 8 - (KW - 1 - j), 0)
        dx_out[ch] = full[8:].astype(BF16)
        edge_out[ch, 0:8] = full[0:8]
        edge_out[ch, 8:16] = full[count : count + 8]
        dw_out[ch] = jnp.concatenate(
            [jnp.sum(dy * taps[ch][j], axis=0, keepdims=True) for j in range(KW)], axis=0
        )


def on_device(conv_inputs, conv_weight, gate_logs, beta_rates, state_resets, out_grad):
    count, channels = gate_logs.shape
    heads = beta_rates.shape[0]
    blocks = state_resets.shape[0]
    x3 = jnp.transpose(conv_inputs, (1, 0, 2))
    w3 = jnp.transpose(conv_weight, (1, 0, 2))
    rim = shifted(x3[:, count - 8 :], "seq", 1)

    smem = pl.BlockSpec(memory_space=pltpu.SMEM)
    tri = lambda n: pl.BlockSpec((3, n, DK), lambda h: (0, 0, h))
    rows = pl.BlockSpec((count, DK), lambda h: (0, h))
    whole = pl.BlockSpec((heads, count), lambda h: (0, 0))
    square = pl.BlockSpec((1, count, count), lambda h: (h, 0, 0))
    per_block = pl.BlockSpec((1, blocks, DK, DK), lambda h: (h, 0, 0, 0))
    per_head = pl.BlockSpec((1, DK, DK), lambda h: (h, 0, 0))
    common_specs = [smem, tri(count), tri(8), tri(KW), rows, whole, rows]
    common = (state_resets, x3, rim, w3, gate_logs, beta_rates, out_grad)
    shape = jax.ShapeDtypeStruct
    params = pltpu.CompilerParams(
        dimension_semantics=("arbitrary",), vmem_limit_bytes=48 * 1024 * 1024
    )
    rows_f32 = shape((count, channels), F32)
    blocks_f32 = shape((heads, blocks, DK, DK), F32)
    head_f32 = shape((heads, DK, DK), F32)
    inv, w, u, pdo, mb, nb, gb, m, n, g = pl.pallas_call(
        maps_kernel,
        grid=(heads,),
        in_specs=common_specs,
        out_specs=[square, rows, rows, rows] + [per_block] * 3 + [per_head] * 3,
        out_shape=[shape((heads, count, count), F32), rows_f32, rows_f32, rows_f32]
        + [blocks_f32] * 3
        + [head_f32] * 3,
        compiler_params=params,
        name="maps",
    )(*common)

    high = lax.Precision.HIGHEST
    steps = lax.axis_size("seq") - 1
    state = shifted(n, "seq", 1)
    grad = shifted(g, "seq", -1)
    for _ in range(steps - 1):
        state_next = jnp.einsum("hij,hjk->hik", m, state, precision=high) + n
        grad_next = jnp.einsum("hji,hjk->hik", m, grad, precision=high) + g
        state = shifted(state_next, "seq", 1)
        grad = shifted(grad_next, "seq", -1)

    dx, dg, db, dw, edge = pl.pallas_call(
        grads_kernel,
        grid=(heads,),
        in_specs=common_specs + [square, rows, rows, rows] + [per_block] * 3 + [per_head] * 2,
        out_specs=[tri(count), rows, whole, tri(KW), tri(16)],
        out_shape=[
            shape(x3.shape, BF16),
            shape((count, channels), BF16),
            shape((heads, count), F32),
            shape(w3.shape, F32),
            shape((3, 16, channels), F32),
        ],
        compiler_params=params,
        name="grads",
    )(*common, inv, w, u, pdo, mb, nb, gb, state, grad)
    spill = shifted(edge[:, :8], "seq", -1)
    dx = dx.at[:, count - 8 :].set((edge[:, 8:] + spill).astype(BF16))
    return (
        jnp.transpose(dx, (1, 0, 2)),
        dg,
        db,
        jnp.transpose(lax.psum(dw, "seq"), (1, 0, 2)),
    )


def solution(mesh):
    in_specs = (
        P(("rep", "seq"), None, ("head", "sub")),
        P(None, None, ("head", "sub")),
        P(("rep", "seq"), ("head", "sub")),
        P(("head", "sub"), ("rep", "seq")),
        P(("rep", "seq")),
        P(("rep", "seq"), ("head", "sub")),
    )
    out_specs = (
        P(("rep", "seq"), None, ("head", "sub")),
        P(("rep", "seq"), ("head", "sub")),
        P(("head", "sub"), ("rep", "seq")),
        P("rep", None, ("head", "sub")),
    )
    return jax.shard_map(
        on_device, mesh=mesh, in_specs=in_specs, out_specs=out_specs, check_vma=False
    )
```

```python
import jax
import jax.numpy as jnp
from jax import lax
from jax.experimental import pallas as pl
from jax.experimental.pallas import tpu as pltpu
from jax.sharding import PartitionSpec as P

DK = 128
KW = 4
BLOCK = 64
SCALE = DK ** (-0.5)
F32 = jnp.float32
BF16 = jnp.bfloat16


def shifted(array, axis, by):
    count = lax.axis_size(axis)
    pairs = [(i, i + by) for i in range(count) if 0 <= i + by < count]
    return lax.ppermute(array, axis, pairs)


def summed(array, axis):
    count = lax.axis_size(axis)
    if count & (count - 1):
        return lax.psum(array, axis)
    step = 1
    while step < count:
        array = array + lax.ppermute(array, axis, [(i, i ^ step) for i in range(count)])
        step *= 2
    return array


def split(a):
    high = a.astype(BF16)
    return (high, (a - high.astype(F32)).astype(BF16))


def dot(a, b, ca, cb):
    return lax.dot_general(a, b, (((ca,), (cb,)), ((), ())), preferred_element_type=F32)


def mm(a, b, ca=1, cb=0):
    out = dot(a[0], b[0], ca, cb)
    if len(b) > 1:
        out = out + dot(a[0], b[1], ca, cb)
    if len(a) > 1:
        out = out + dot(a[1], b[0], ca, cb)
    return out


def rows_of(a, b):
    return tuple(p[b * BLOCK : (b + 1) * BLOCK] for p in a)


def positions(count):
    r = lax.broadcasted_iota(jnp.int32, (count, count), 0)
    c = lax.broadcasted_iota(jnp.int32, (count, count), 1)
    return r, c, jnp.bitwise_xor(r, c)


def column(row):
    return jnp.transpose(jnp.broadcast_to(row, (DK, row.shape[1])))


def local_terms(x_ref, rim_ref, w_ref, g_ref, upto):
    count = x_ref.shape[1]
    taps, mixed, sigs, acts = [], [], [], []
    for c in range(3):
        ext = jnp.concatenate([rim_ref[c].astype(F32), x_ref[c].astype(F32)], axis=0)
        rolled = [pltpu.roll(ext, KW - 1 - j, 0)[8:] if j < KW - 1 else ext[8:] for j in range(KW)]
        y = w_ref[c, 0:1] * rolled[0]
        for j in range(1, KW):
            y = y + w_ref[c, j : j + 1] * rolled[j]
        sig = 1.0 / (1.0 + jnp.exp(-y))
        taps.append(rolled)
        mixed.append(y)
        sigs.append(sig)
        acts.append(y * sig)
    rq = lax.rsqrt(jnp.sum(acts[0] * acts[0], axis=1, keepdims=True) + 1e-6)
    rk = lax.rsqrt(jnp.sum(acts[1] * acts[1], axis=1, keepdims=True) + 1e-6)
    q = acts[0] * rq * SCALE
    k = acts[1] * rk
    decays = dot(upto, g_ref[...], 1, 0)
    ends = [decays[b * BLOCK + BLOCK - 1 : (b + 1) * BLOCK] for b in range(count // BLOCK)]
    last = jnp.concatenate([jnp.broadcast_to(e, (BLOCK, DK)) for e in ends], axis=0)
    return taps, mixed, sigs, acts, rq, rk, q, k, decays, last, ends


def maps_kernel(
    resets_ref, x_ref, rim_ref, w_ref, g_ref, beta_ref, do_ref,
    x_out, w_out, u_out, pdo_out, mb_out, nb_out, gb_out, m_out, n_out, g_out,
):
    count = x_ref.shape[1]
    blocks = count // BLOCK
    group = x_out.shape[0]
    r, c, x = positions(count)
    inside = x < BLOCK
    upto_mask = inside & (r >= c)
    upto = upto_mask.astype(F32).astype(BF16)
    lower = r > c
    parts, ns, invs = [], [], []
    for i in range(group):
        lanes = pl.ds(i * DK, DK)
        taps, mixed, sigs, acts, rq, rk, q, k, decays, last, ends = local_terms(
            x_ref.at[:, :, lanes],
            rim_ref.at[:, :, lanes],
            w_ref.at[:, :, lanes],
            g_ref.at[:, lanes],
            upto,
        )
        grow = jnp.exp(decays)
        kp = k * grow
        km = split(k * jnp.exp(-decays))
        qb = split(q * grow)
        kf = split(k * jnp.exp(last - decays))
        beta = column(beta_ref[pl.ds(pl.program_id(0) * group + i, 1), :])
        wide = jnp.concatenate([beta] * (count // DK), axis=1)
        n = mm(split(kp), km, 1, 1) * wide
        right = jnp.concatenate([beta * acts[2], beta * kp], axis=1)
        parts.append((km, qb, kf, right, ends))
        ns.append(n)
        invs.append(jnp.where(r == c, 1.0, 0.0) - jnp.where(lower & (x < 2) & (x >= 1), n, 0.0))
    s = 2
    while s < BLOCK:
        here = lower & (x >= s) & (x < 2 * s)
        inv_s = [split(inv) for inv in invs]
        half = [mm(inv_s[i], split(jnp.where(here, ns[i], 0.0))) for i in range(group)]
        invs = [invs[i] - mm(split(half[i]), inv_s[i]) for i in range(group)]
        s *= 2
    er = lax.broadcasted_iota(jnp.int32, (DK, DK), 0) == lax.broadcasted_iota(jnp.int32, (DK, DK), 1)
    keeps = [1.0 - resets_ref[b].astype(F32) for b in range(blocks)]
    ms, nbs, gs = [], [], []
    for i in range(group):
        km, qb, kf, right, ends = parts[i]
        lanes = pl.ds(i * DK, DK)
        x_out[i] = invs[i]
        both = mm(split(invs[i]), split(right))
        u_out[:, lanes] = both[:, :DK]
        w_out[:, lanes] = both[:, DK:]
        do = (do_ref[:, lanes],)
        p = split(jnp.where(upto_mask, mm(qb, km, 1, 1), 0.0))
        pdo = mm(p, do, 0, 0)
        pdo_out[:, lanes] = pdo
        both_s = split(both)
        pdo_s = split(pdo)
        w_s = tuple(a[:, DK:] for a in both_s)
        m_list, n_list, g_list = [], [], []
        for b in range(blocks):
            nm = mm(rows_of(kf, b), rows_of(both_s, b), 0, 0)
            m = (jnp.where(er, jnp.exp(ends[b]), 0.0) - nm[:, DK:]) * keeps[b]
            g = mm(rows_of(qb, b), rows_of(do, b), 0, 0) - mm(
                rows_of(w_s, b), rows_of(pdo_s, b), 0, 0
            )
            g = g * keeps[b]
            mb_out[i, b] = m
            nb_out[i, b] = nm[:, :DK]
            gb_out[i, b] = g
            m_list.append((m, split(m)))
            n_list.append(nm[:, :DK])
            g_list.append(g)
        ms.append(m_list)
        nbs.append(n_list)
        gs.append(g_list)
    accs = [jnp.concatenate([ms[i][0][0], nbs[i][0]], axis=1) for i in range(group)]
    grads = [gs[i][-1] for i in range(group)]
    for b in range(1, blocks):
        back = blocks - 1 - b
        for i in range(group):
            acc = mm(ms[i][b][1], split(accs[i]))
            accs[i] = jnp.concatenate([acc[:, :DK], acc[:, DK:] + nbs[i][b]], axis=1)
            grads[i] = mm(ms[i][back][1], split(grads[i]), 0, 0) + gs[i][back]
    for i in range(group):
        m_out[i] = accs[i][:, :DK]
        n_out[i] = accs[i][:, DK:]
        g_out[i] = grads[i]


def grads_kernel(
    resets_ref, x_ref, rim_ref, w_ref, g_ref, beta_ref, do_ref,
    inv_ref, wm_ref, u_ref, pdo_ref, mb_ref, nb_ref, gb_ref, s_ref, ds_ref,
    dx_out, dg_out, db_out, dw_out, edge_out,
):
    count = x_ref.shape[1]
    blocks = count // BLOCK
    r, c, x = positions(count)
    inside = x < BLOCK
    upto_mask = inside & (r >= c)
    upto = upto_mask.astype(F32).astype(BF16)
    taps, mixed, sigs, acts, rq, rk, q, k, decays, last, ends = local_terms(
        x_ref, rim_ref, w_ref, g_ref, upto
    )
    v = acts[2]
    grow = jnp.exp(decays)
    shrink = jnp.exp(-decays)
    tail = jnp.exp(last - decays)
    kp, km, qb, kf = k * grow, k * shrink, q * grow, k * tail
    kp_s, km_s, qb_s, kf_s = split(kp), split(km), split(qb), split(kf)
    beta = column(beta_ref[pl.ds(pl.program_id(0), 1), :])
    do = do_ref[...]

    ms = [split(mb_ref[0, b]) for b in range(blocks)]
    states = []
    now = s_ref[0]
    for b in range(blocks):
        states.append(now * (1.0 - resets_ref[b].astype(F32)))
        if b < blocks - 1:
            now = mm(ms[b], split(now)) + nb_ref[0, b]
    states_s = [split(a) for a in states]
    after = [None] * blocks
    after[-1] = ds_ref[0]
    for b in range(blocks - 1, 0, -1):
        after[b - 1] = mm(ms[b], split(after[b]), 0, 0) + gb_ref[0, b]
    after_s = [split(a) for a in after]

    w_s = split(wm_ref[...])
    u = u_ref[...] - jnp.concatenate([mm(rows_of(w_s, b), states_s[b]) for b in range(blocks)], axis=0)
    u_s = split(u)
    du = pdo_ref[...] + jnp.concatenate([mm(rows_of(kf_s, b), after_s[b]) for b in range(blocks)], axis=0)
    drv = mm(split(inv_ref[0]), split(du), 0, 0)
    drv_s = split(drv)
    do_s = (do,)
    dp_s = split(jnp.where(upto_mask, mm(do_s, u_s, 1, 1), 0.0))
    dt = jnp.where(inside & (r > c), mm(drv_s, u_s, 1, 1), 0.0)
    dt_s = split(-dt)
    dq_state, drw, dkf, extra = [], [], [], []
    ones = (jnp.ones((8, DK), BF16),)
    for b in range(blocks):
        dq_state.append(mm(rows_of(do_s, b), states_s[b], 1, 1))
        drw.append(-mm(rows_of(drv_s, b), states_s[b], 1, 1))
        dkf.append(mm(rows_of(u_s, b), after_s[b], 1, 1))
        extra.append(mm(ones, split(states[b] * after[b]), 1, 1)[0:1] * jnp.exp(ends[b]))
    dqb = jnp.concatenate(dq_state, axis=0) + mm(dp_s, km_s)
    inner = jnp.concatenate(drw, axis=0) + mm(dt_s, km_s)
    dkf = jnp.concatenate(dkf, axis=0)
    dkp = beta * inner
    wide = jnp.concatenate([beta] * (count // DK), axis=1)
    da_s = split(-dt * wide)
    dkm = mm(dp_s, qb_s, 0, 0) + mm(da_s, kp_s, 0, 0)
    dbeta = jnp.sum(drv * v + kp * inner, axis=1, keepdims=True)
    db_out[pl.ds(pl.program_id(0), 1), :] = jnp.transpose(jnp.broadcast_to(dbeta, (count, DK)))[0:1]

    through = dkf * kf
    dd = dkp * kp - dkm * km - through + dqb * qb
    dg = mm((upto,), split(dd), 0, 0)
    whole = []
    for b in range(blocks):
        total = jnp.sum(through[b * BLOCK : (b + 1) * BLOCK], axis=0, keepdims=True) + extra[b]
        whole.append(jnp.broadcast_to(total, (BLOCK, DK)))
    dg_out[...] = (dg + jnp.concatenate(whole, axis=0)).astype(BF16)

    dq = dqb * grow
    dk = dkp * grow + dkm * shrink + dkf * tail
    dv = beta * drv
    da_q = SCALE * rq * dq - acts[0] * (rq * rq) * jnp.sum(q * dq, axis=1, keepdims=True)
    da_k = rk * dk - acts[1] * (rk * rk) * jnp.sum(k * dk, axis=1, keepdims=True)
    zeros = jnp.zeros((8, DK), F32)
    for ch, da in enumerate((da_q, da_k, dv)):
        dy = da * sigs[ch] * (1.0 + mixed[ch] * (1.0 - sigs[ch]))
        ext = jnp.concatenate([zeros, dy], axis=0)
        full = w_ref[ch, KW - 1 : KW] * ext
        for j in range(KW - 1):
            full = full + w_ref[ch, j : j + 1] * pltpu.roll(ext, count + 8 - (KW - 1 - j), 0)
        dx_out[ch] = full[8:].astype(BF16)
        edge_out[ch, 0:8] = full[0:8]
        edge_out[ch, 8:16] = full[count : count + 8]
        dw_out[ch] = jnp.concatenate(
            [jnp.sum(dy * taps[ch][j], axis=0, keepdims=True) for j in range(KW)], axis=0
        )


def on_device(conv_inputs, conv_weight, gate_logs, beta_rates, state_resets, out_grad):
    count, channels = gate_logs.shape
    heads = beta_rates.shape[0]
    blocks = state_resets.shape[0]
    x3 = jnp.transpose(conv_inputs, (1, 0, 2))
    w3 = jnp.transpose(conv_weight, (1, 0, 2))
    rim = shifted(x3[:, count - 8 :], "seq", 1)

    smem = pl.BlockSpec(memory_space=pltpu.SMEM)
    tri = lambda n: pl.BlockSpec((3, n, DK), lambda h: (0, 0, h))
    rows = pl.BlockSpec((count, DK), lambda h: (0, h))
    whole = pl.BlockSpec((heads, count), lambda h: (0, 0))
    square = pl.BlockSpec((1, count, count), lambda h: (h, 0, 0))
    per_block = pl.BlockSpec((1, blocks, DK, DK), lambda h: (h, 0, 0, 0))
    per_head = pl.BlockSpec((1, DK, DK), lambda h: (h, 0, 0))
    common_specs = [smem, tri(count), tri(8), tri(KW), rows, whole, rows]
    common = (state_resets, x3, rim, w3, gate_logs, beta_rates, out_grad)
    shape = jax.ShapeDtypeStruct
    params = pltpu.CompilerParams(
        dimension_semantics=("arbitrary",), vmem_limit_bytes=48 * 1024 * 1024
    )
    rows_f32 = shape((count, channels), F32)
    blocks_f32 = shape((heads, blocks, DK, DK), F32)
    head_f32 = shape((heads, DK, DK), F32)
    group = 2 if heads % 2 == 0 else 1
    tri_g = lambda n: pl.BlockSpec((3, n, group * DK), lambda h: (0, 0, h))
    rows_g = pl.BlockSpec((count, group * DK), lambda h: (0, h))
    square_g = pl.BlockSpec((group, count, count), lambda h: (h, 0, 0))
    per_block_g = pl.BlockSpec((group, blocks, DK, DK), lambda h: (h, 0, 0, 0))
    per_head_g = pl.BlockSpec((group, DK, DK), lambda h: (h, 0, 0))
    inv, w, u, pdo, mb, nb, gb, m, n, g = pl.pallas_call(
        maps_kernel,
        grid=(heads // group,),
        in_specs=[smem, tri_g(count), tri_g(8), tri_g(KW), rows_g, whole, rows_g],
        out_specs=[square_g, rows_g, rows_g, rows_g] + [per_block_g] * 3 + [per_head_g] * 3,
        out_shape=[shape((heads, count, count), F32), rows_f32, rows_f32, rows_f32]
        + [blocks_f32] * 3
        + [head_f32] * 3,
        compiler_params=params,
        name="maps",
    )(*common)

    high = lax.Precision.HIGHEST
    steps = lax.axis_size("seq") - 1
    state = shifted(n, "seq", 1)
    grad = shifted(g, "seq", -1)
    for _ in range(steps - 1):
        state_next = jnp.einsum("hij,hjk->hik", m, state, precision=high) + n
        grad_next = jnp.einsum("hji,hjk->hik", m, grad, precision=high) + g
        state = shifted(state_next, "seq", 1)
        grad = shifted(grad_next, "seq", -1)

    dx, dg, db, dw, edge = pl.pallas_call(
        grads_kernel,
        grid=(heads,),
        in_specs=common_specs + [square, rows, rows, rows] + [per_block] * 3 + [per_head] * 2,
        out_specs=[tri(count), rows, whole, tri(KW), tri(16)],
        out_shape=[
            shape(x3.shape, BF16),
            shape((count, channels), BF16),
            shape((heads, count), F32),
            shape(w3.shape, F32),
            shape((3, 16, channels), F32),
        ],
        compiler_params=params,
        name="grads",
    )(*common, inv, w, u, pdo, mb, nb, gb, state, grad)
    spill = shifted(edge[:, :8], "seq", -1)
    dx = dx.at[:, count - 8 :].set((edge[:, 8:] + spill).astype(BF16))
    return (
        jnp.transpose(dx, (1, 0, 2)),
        dg,
        db,
        jnp.transpose(summed(dw, "seq"), (1, 0, 2)),
    )


def solution(mesh):
    in_specs = (
        P(("rep", "seq"), None, ("head", "sub")),
        P(None, None, ("head", "sub")),
        P(("rep", "seq"), ("head", "sub")),
        P(("head", "sub"), ("rep", "seq")),
        P(("rep", "seq")),
        P(("rep", "seq"), ("head", "sub")),
    )
    out_specs = (
        P(("rep", "seq"), None, ("head", "sub")),
        P(("rep", "seq"), ("head", "sub")),
        P(("head", "sub"), ("rep", "seq")),
        P("rep", None, ("head", "sub")),
    )
    return jax.shard_map(
        on_device, mesh=mesh, in_specs=in_specs, out_specs=out_specs, check_vma=False
    )
```

```python
import jax
import jax.numpy as jnp
from jax import lax
from jax.experimental import pallas as pl
from jax.experimental.pallas import tpu as pltpu
from jax.sharding import PartitionSpec as P

DK = 128
KW = 4
BLOCK = 64
SCALE = DK ** (-0.5)
F32 = jnp.float32
BF16 = jnp.bfloat16


def shifted(array, axis, by):
    count = lax.axis_size(axis)
    pairs = [(i, i + by) for i in range(count) if 0 <= i + by < count]
    return lax.ppermute(array, axis, pairs)


def summed(array, axis):
    count = lax.axis_size(axis)
    if count & (count - 1):
        return lax.psum(array, axis)
    step = 1
    while step < count:
        array = array + lax.ppermute(array, axis, [(i, i ^ step) for i in range(count)])
        step *= 2
    return array


def split(a):
    high = a.astype(BF16)
    return (high, (a - high.astype(F32)).astype(BF16))


def dot(a, b, ca, cb):
    return lax.dot_general(a, b, (((ca,), (cb,)), ((), ())), preferred_element_type=F32)


def mm(a, b, ca=1, cb=0):
    out = dot(a[0], b[0], ca, cb)
    if len(b) > 1:
        out = out + dot(a[0], b[1], ca, cb)
    if len(a) > 1:
        out = out + dot(a[1], b[0], ca, cb)
    return out


def rows_of(a, b):
    return tuple(p[b * BLOCK : (b + 1) * BLOCK] for p in a)


def positions(count):
    r = lax.broadcasted_iota(jnp.int32, (count, count), 0)
    c = lax.broadcasted_iota(jnp.int32, (count, count), 1)
    return r, c, jnp.bitwise_xor(r, c)


def column(row):
    return jnp.transpose(jnp.broadcast_to(row, (DK, row.shape[1])))


def local_terms(x_ref, rim_ref, w_ref, g_ref, upto):
    count = x_ref.shape[1]
    taps, mixed, sigs, acts = [], [], [], []
    for c in range(3):
        ext = jnp.concatenate([rim_ref[c].astype(F32), x_ref[c].astype(F32)], axis=0)
        rolled = [pltpu.roll(ext, KW - 1 - j, 0)[8:] if j < KW - 1 else ext[8:] for j in range(KW)]
        y = w_ref[c, 0:1] * rolled[0]
        for j in range(1, KW):
            y = y + w_ref[c, j : j + 1] * rolled[j]
        sig = 1.0 / (1.0 + jnp.exp(-y))
        taps.append(rolled)
        mixed.append(y)
        sigs.append(sig)
        acts.append(y * sig)
    rq = lax.rsqrt(jnp.sum(acts[0] * acts[0], axis=1, keepdims=True) + 1e-6)
    rk = lax.rsqrt(jnp.sum(acts[1] * acts[1], axis=1, keepdims=True) + 1e-6)
    q = acts[0] * rq * SCALE
    k = acts[1] * rk
    decays = dot(upto, g_ref[...], 1, 0)
    ends = [decays[b * BLOCK + BLOCK - 1 : (b + 1) * BLOCK] for b in range(count // BLOCK)]
    last = jnp.concatenate([jnp.broadcast_to(e, (BLOCK, DK)) for e in ends], axis=0)
    return taps, mixed, sigs, acts, rq, rk, q, k, decays, last, ends


def maps_kernel(
    resets_ref, x_ref, rim_ref, w_ref, g_ref, beta_ref, do_ref,
    x_out, w_out, u_out, pdo_out, mb_out, nb_out, gb_out, m_out, n_out, g_out,
):
    count = x_ref.shape[1]
    blocks = count // BLOCK
    group = x_out.shape[0]
    r, c, x = positions(count)
    inside = x < BLOCK
    upto_mask = inside & (r >= c)
    upto = upto_mask.astype(F32).astype(BF16)
    lower = r > c
    parts, ns, invs = [], [], []
    for i in range(group):
        lanes = pl.ds(i * DK, DK)
        taps, mixed, sigs, acts, rq, rk, q, k, decays, last, ends = local_terms(
            x_ref.at[:, :, lanes],
            rim_ref.at[:, :, lanes],
            w_ref.at[:, :, lanes],
            g_ref.at[:, lanes],
            upto,
        )
        grow = jnp.exp(decays)
        kp = k * grow
        km = split(k * jnp.exp(-decays))
        qb = split(q * grow)
        kf = split(k * jnp.exp(last - decays))
        beta = column(beta_ref[pl.ds(pl.program_id(0) * group + i, 1), :])
        wide = jnp.concatenate([beta] * (count // DK), axis=1)
        n = mm(split(kp), km, 1, 1) * wide
        right = jnp.concatenate([beta * acts[2], beta * kp], axis=1)
        parts.append((km, qb, kf, right, ends))
        ns.append(n)
        invs.append(jnp.where(r == c, 1.0, 0.0) - jnp.where(lower & (x < 2) & (x >= 1), n, 0.0))
    s = 2
    while s < BLOCK:
        here = lower & (x >= s) & (x < 2 * s)
        inv_s = [split(inv) for inv in invs]
        half = [mm(inv_s[i], split(jnp.where(here, ns[i], 0.0))) for i in range(group)]
        invs = [invs[i] - mm(split(half[i]), inv_s[i]) for i in range(group)]
        s *= 2
    er = lax.broadcasted_iota(jnp.int32, (DK, DK), 0) == lax.broadcasted_iota(jnp.int32, (DK, DK), 1)
    keeps = [1.0 - resets_ref[b].astype(F32) for b in range(blocks)]
    ms, nbs, gs = [], [], []
    for i in range(group):
        km, qb, kf, right, ends = parts[i]
        lanes = pl.ds(i * DK, DK)
        x_out[i] = invs[i]
        both = mm(split(invs[i]), split(right))
        u_out[:, lanes] = both[:, :DK]
        w_out[:, lanes] = both[:, DK:]
        do = (do_ref[:, lanes],)
        p = split(jnp.where(upto_mask, mm(qb, km, 1, 1), 0.0))
        pdo = mm(p, do, 0, 0)
        pdo_out[:, lanes] = pdo
        both_s = split(both)
        pdo_s = split(pdo)
        w_s = tuple(a[:, DK:] for a in both_s)
        m_list, n_list, g_list = [], [], []
        for b in range(blocks):
            nm = mm(rows_of(kf, b), rows_of(both_s, b), 0, 0)
            m = (jnp.where(er, jnp.exp(ends[b]), 0.0) - nm[:, DK:]) * keeps[b]
            g = mm(rows_of(qb, b), rows_of(do, b), 0, 0) - mm(
                rows_of(w_s, b), rows_of(pdo_s, b), 0, 0
            )
            g = g * keeps[b]
            mb_out[i, b] = m
            nb_out[i, b] = nm[:, :DK]
            gb_out[i, b] = g
            m_list.append((m, split(m)))
            n_list.append(nm[:, :DK])
            g_list.append(g)
        ms.append(m_list)
        nbs.append(n_list)
        gs.append(g_list)
    accs = [jnp.concatenate([ms[i][0][0], nbs[i][0]], axis=1) for i in range(group)]
    grads = [gs[i][-1] for i in range(group)]
    for b in range(1, blocks):
        back = blocks - 1 - b
        for i in range(group):
            acc = mm(ms[i][b][1], split(accs[i]))
            accs[i] = jnp.concatenate([acc[:, :DK], acc[:, DK:] + nbs[i][b]], axis=1)
            grads[i] = mm(ms[i][back][1], split(grads[i]), 0, 0) + gs[i][back]
    for i in range(group):
        m_out[i] = accs[i][:, :DK]
        n_out[i] = accs[i][:, DK:]
        g_out[i] = grads[i]


def grads_kernel(
    resets_ref, x_ref, rim_ref, w_ref, g_ref, beta_ref, do_ref,
    inv_ref, wm_ref, u_ref, pdo_ref, mb_ref, nb_ref, gb_ref, s_ref, ds_ref,
    dx_out, dg_out, db_out, dw_out, edge_out,
):
    count = x_ref.shape[1]
    blocks = count // BLOCK
    r, c, x = positions(count)
    inside = x < BLOCK
    upto_mask = inside & (r >= c)
    upto = upto_mask.astype(F32).astype(BF16)
    taps, mixed, sigs, acts, rq, rk, q, k, decays, last, ends = local_terms(
        x_ref, rim_ref, w_ref, g_ref, upto
    )
    v = acts[2]
    grow = jnp.exp(decays)
    shrink = jnp.exp(-decays)
    tail = jnp.exp(last - decays)
    kp, km, qb, kf = k * grow, k * shrink, q * grow, k * tail
    kp_s, km_s, qb_s, kf_s = split(kp), split(km), split(qb), split(kf)
    beta = column(beta_ref[pl.ds(pl.program_id(0), 1), :])
    do = do_ref[...]

    ms = [split(mb_ref[0, b]) for b in range(blocks)]
    states = []
    now = s_ref[0]
    for b in range(blocks):
        states.append(now * (1.0 - resets_ref[b].astype(F32)))
        if b < blocks - 1:
            now = mm(ms[b], split(now)) + nb_ref[0, b]
    states_s = [split(a) for a in states]
    after = [None] * blocks
    after[-1] = ds_ref[0]
    for b in range(blocks - 1, 0, -1):
        after[b - 1] = mm(ms[b], split(after[b]), 0, 0) + gb_ref[0, b]
    after_s = [split(a) for a in after]

    w_s = split(wm_ref[...])
    u = u_ref[...] - jnp.concatenate([mm(rows_of(w_s, b), states_s[b]) for b in range(blocks)], axis=0)
    u_s = split(u)
    du = pdo_ref[...] + jnp.concatenate([mm(rows_of(kf_s, b), after_s[b]) for b in range(blocks)], axis=0)
    drv = mm(split(inv_ref[0]), split(du), 0, 0)
    drv_s = split(drv)
    do_s = (do,)
    dp_s = split(jnp.where(upto_mask, mm(do_s, u_s, 1, 1), 0.0))
    dt = jnp.where(inside & (r > c), mm(drv_s, u_s, 1, 1), 0.0)
    dt_s = split(-dt)
    dq_state, drw, dkf, extra = [], [], [], []
    ones = (jnp.ones((8, DK), BF16),)
    for b in range(blocks):
        dq_state.append(mm(rows_of(do_s, b), states_s[b], 1, 1))
        drw.append(-mm(rows_of(drv_s, b), states_s[b], 1, 1))
        dkf.append(mm(rows_of(u_s, b), after_s[b], 1, 1))
        extra.append(mm(ones, split(states[b] * after[b]), 1, 1)[0:1] * jnp.exp(ends[b]))
    dqb = jnp.concatenate(dq_state, axis=0) + mm(dp_s, km_s)
    inner = jnp.concatenate(drw, axis=0) + mm(dt_s, km_s)
    dkf = jnp.concatenate(dkf, axis=0)
    dkp = beta * inner
    wide = jnp.concatenate([beta] * (count // DK), axis=1)
    da_s = split(-dt * wide)
    dkm = mm(dp_s, qb_s, 0, 0) + mm(da_s, kp_s, 0, 0)
    dbeta = jnp.sum(drv * v + kp * inner, axis=1, keepdims=True)
    db_out[pl.ds(pl.program_id(0), 1), :] = jnp.transpose(jnp.broadcast_to(dbeta, (count, DK)))[0:1]

    through = dkf * kf
    dd = dkp * kp - dkm * km - through + dqb * qb
    dg = mm((upto,), split(dd), 0, 0)
    whole = []
    for b in range(blocks):
        total = jnp.sum(through[b * BLOCK : (b + 1) * BLOCK], axis=0, keepdims=True) + extra[b]
        whole.append(jnp.broadcast_to(total, (BLOCK, DK)))
    dg_out[...] = (dg + jnp.concatenate(whole, axis=0)).astype(BF16)

    dq = dqb * grow
    dk = dkp * grow + dkm * shrink + dkf * tail
    dv = beta * drv
    da_q = SCALE * rq * dq - acts[0] * (rq * rq) * jnp.sum(q * dq, axis=1, keepdims=True)
    da_k = rk * dk - acts[1] * (rk * rk) * jnp.sum(k * dk, axis=1, keepdims=True)
    zeros = jnp.zeros((8, DK), F32)
    for ch, da in enumerate((da_q, da_k, dv)):
        dy = da * sigs[ch] * (1.0 + mixed[ch] * (1.0 - sigs[ch]))
        ext = jnp.concatenate([zeros, dy], axis=0)
        full = w_ref[ch, KW - 1 : KW] * ext
        for j in range(KW - 1):
            full = full + w_ref[ch, j : j + 1] * pltpu.roll(ext, count + 8 - (KW - 1 - j), 0)
        dx_out[ch] = full[8:].astype(BF16)
        edge_out[ch, 0:8] = full[0:8]
        edge_out[ch, 8:16] = full[count : count + 8]
        dw_out[ch] = jnp.concatenate(
            [jnp.sum(dy * taps[ch][j], axis=0, keepdims=True) for j in range(KW)], axis=0
        )


def chain_kernel(
    m_ref, n_ref, g_ref, state_out, grad_out,
    state, grad, send_f, send_b, f_sent, f_got, b_sent, b_got,
):
    heads = m_ref.shape[0]
    place = lax.axis_index("seq")
    count = lax.axis_size("seq")
    has_next = place < count - 1
    has_prev = place > 0
    after = {"seq": jnp.minimum(place + 1, count - 1)}
    before = {"seq": jnp.maximum(place - 1, 0)}
    mesh_ids = pl.DeviceIdType.MESH

    def forward(h, to):
        return pltpu.make_async_remote_copy(
            send_f.at[h], state.at[h], f_sent.at[h], f_got.at[h], to, mesh_ids
        )

    def backward(h, to):
        return pltpu.make_async_remote_copy(
            send_b.at[h], grad.at[h], b_sent.at[h], b_got.at[h], to, mesh_ids
        )

    barrier = pltpu.get_barrier_semaphore()

    @pl.when(has_next)
    def _():
        pl.semaphore_signal(barrier, inc=1, device_id=after, device_id_type=mesh_ids)

    @pl.when(has_prev)
    def _():
        pl.semaphore_signal(barrier, inc=1, device_id=before, device_id_type=mesh_ids)

    pl.semaphore_wait(barrier, has_next.astype(jnp.int32) + has_prev.astype(jnp.int32))

    @pl.when(place == 0)
    def _():
        state[...] = jnp.zeros_like(state)

    @pl.when(place == count - 1)
    def _():
        grad[...] = jnp.zeros_like(grad)

    def turn(t, carry):
        hf = t - place
        hb = t - (count - 1 - place)

        @pl.when((hf >= 0) & (hf < heads))
        def _():
            @pl.when(has_prev)
            def _():
                forward(hf, before).wait_recv()

            @pl.when(has_next)
            def _():
                send_f[hf] = mm(split(m_ref[hf]), split(state[hf])) + n_ref[hf]
                forward(hf, after).start()

        @pl.when((hb >= 0) & (hb < heads))
        def _():
            @pl.when(has_next)
            def _():
                backward(hb, after).wait_recv()

            @pl.when(has_prev)
            def _():
                send_b[hb] = mm(split(m_ref[hb]), split(grad[hb]), 0, 0) + g_ref[hb]
                backward(hb, before).start()

        return carry

    lax.fori_loop(0, heads + count - 1, turn, 0)

    def finish(h, carry):
        @pl.when(has_next)
        def _():
            forward(h, after).wait_send()

        @pl.when(has_prev)
        def _():
            backward(h, before).wait_send()

        return carry

    lax.fori_loop(0, heads, finish, 0)
    state_out[...] = state[...]
    grad_out[...] = grad[...]


def on_device(conv_inputs, conv_weight, gate_logs, beta_rates, state_resets, out_grad):
    count, channels = gate_logs.shape
    heads = beta_rates.shape[0]
    blocks = state_resets.shape[0]
    x3 = jnp.transpose(conv_inputs, (1, 0, 2))
    w3 = jnp.transpose(conv_weight, (1, 0, 2))
    rim = shifted(x3[:, count - 8 :], "seq", 1)

    smem = pl.BlockSpec(memory_space=pltpu.SMEM)
    tri = lambda n: pl.BlockSpec((3, n, DK), lambda h: (0, 0, h))
    rows = pl.BlockSpec((count, DK), lambda h: (0, h))
    whole = pl.BlockSpec((heads, count), lambda h: (0, 0))
    square = pl.BlockSpec((1, count, count), lambda h: (h, 0, 0))
    per_block = pl.BlockSpec((1, blocks, DK, DK), lambda h: (h, 0, 0, 0))
    per_head = pl.BlockSpec((1, DK, DK), lambda h: (h, 0, 0))
    common_specs = [smem, tri(count), tri(8), tri(KW), rows, whole, rows]
    common = (state_resets, x3, rim, w3, gate_logs, beta_rates, out_grad)
    shape = jax.ShapeDtypeStruct
    params = pltpu.CompilerParams(
        dimension_semantics=("arbitrary",), vmem_limit_bytes=48 * 1024 * 1024
    )
    rows_f32 = shape((count, channels), F32)
    blocks_f32 = shape((heads, blocks, DK, DK), F32)
    head_f32 = shape((heads, DK, DK), F32)
    group = 2 if heads % 2 == 0 else 1
    tri_g = lambda n: pl.BlockSpec((3, n, group * DK), lambda h: (0, 0, h))
    rows_g = pl.BlockSpec((count, group * DK), lambda h: (0, h))
    square_g = pl.BlockSpec((group, count, count), lambda h: (h, 0, 0))
    per_block_g = pl.BlockSpec((group, blocks, DK, DK), lambda h: (h, 0, 0, 0))
    per_head_g = pl.BlockSpec((group, DK, DK), lambda h: (h, 0, 0))
    inv, w, u, pdo, mb, nb, gb, m, n, g = pl.pallas_call(
        maps_kernel,
        grid=(heads // group,),
        in_specs=[smem, tri_g(count), tri_g(8), tri_g(KW), rows_g, whole, rows_g],
        out_specs=[square_g, rows_g, rows_g, rows_g] + [per_block_g] * 3 + [per_head_g] * 3,
        out_shape=[shape((heads, count, count), F32), rows_f32, rows_f32, rows_f32]
        + [blocks_f32] * 3
        + [head_f32] * 3,
        compiler_params=params,
        name="maps",
    )(*common)

    vmem = pl.BlockSpec(memory_space=pltpu.VMEM)
    held = pltpu.VMEM((heads, DK, DK), F32)
    flags = pltpu.SemaphoreType.DMA((heads,))
    state, grad = pl.pallas_call(
        chain_kernel,
        in_specs=[vmem] * 3,
        out_specs=[vmem] * 2,
        out_shape=[head_f32] * 2,
        scratch_shapes=[held] * 4 + [flags] * 4,
        compiler_params=pltpu.CompilerParams(
            collective_id=0, has_side_effects=True, vmem_limit_bytes=32 * 1024 * 1024
        ),
        name="chain",
    )(m, n, g)

    dx, dg, db, dw, edge = pl.pallas_call(
        grads_kernel,
        grid=(heads,),
        in_specs=common_specs + [square, rows, rows, rows] + [per_block] * 3 + [per_head] * 2,
        out_specs=[tri(count), rows, whole, tri(KW), tri(16)],
        out_shape=[
            shape(x3.shape, BF16),
            shape((count, channels), BF16),
            shape((heads, count), F32),
            shape(w3.shape, F32),
            shape((3, 16, channels), F32),
        ],
        compiler_params=params,
        name="grads",
    )(*common, inv, w, u, pdo, mb, nb, gb, state, grad)
    spill = shifted(edge[:, :8], "seq", -1)
    dx = dx.at[:, count - 8 :].set((edge[:, 8:] + spill).astype(BF16))
    return (
        jnp.transpose(dx, (1, 0, 2)),
        dg,
        db,
        jnp.transpose(summed(dw, "seq"), (1, 0, 2)),
    )


def solution(mesh):
    in_specs = (
        P(("rep", "seq"), None, ("head", "sub")),
        P(None, None, ("head", "sub")),
        P(("rep", "seq"), ("head", "sub")),
        P(("head", "sub"), ("rep", "seq")),
        P(("rep", "seq")),
        P(("rep", "seq"), ("head", "sub")),
    )
    out_specs = (
        P(("rep", "seq"), None, ("head", "sub")),
        P(("rep", "seq"), ("head", "sub")),
        P(("head", "sub"), ("rep", "seq")),
        P("rep", None, ("head", "sub")),
    )
    return jax.shard_map(
        on_device, mesh=mesh, in_specs=in_specs, out_specs=out_specs, check_vma=False
    )
```

```python
import jax
import jax.numpy as jnp
from jax import lax
from jax.experimental import pallas as pl
from jax.experimental.pallas import tpu as pltpu
from jax.sharding import PartitionSpec as P

DK = 128
KW = 4
BLOCK = 64
SCALE = DK ** (-0.5)
F32 = jnp.float32
BF16 = jnp.bfloat16


def shifted(array, axis, by):
    count = lax.axis_size(axis)
    pairs = [(i, i + by) for i in range(count) if 0 <= i + by < count]
    return lax.ppermute(array, axis, pairs)


def summed(array, axis):
    count = lax.axis_size(axis)
    if count & (count - 1):
        return lax.psum(array, axis)
    step = 1
    while step < count:
        array = array + lax.ppermute(array, axis, [(i, i ^ step) for i in range(count)])
        step *= 2
    return array


def split(a):
    high = a.astype(BF16)
    return (high, (a - high.astype(F32)).astype(BF16))


def dot(a, b, ca, cb):
    return lax.dot_general(a, b, (((ca,), (cb,)), ((), ())), preferred_element_type=F32)


def mm(a, b, ca=1, cb=0):
    out = dot(a[0], b[0], ca, cb)
    if len(b) > 1:
        out = out + dot(a[0], b[1], ca, cb)
    if len(a) > 1:
        out = out + dot(a[1], b[0], ca, cb)
    return out


def rows_of(a, b):
    return tuple(p[b * BLOCK : (b + 1) * BLOCK] for p in a)


def positions(count):
    r = lax.broadcasted_iota(jnp.int32, (count, count), 0)
    c = lax.broadcasted_iota(jnp.int32, (count, count), 1)
    return r, c, jnp.bitwise_xor(r, c)


def column(row):
    return jnp.transpose(jnp.broadcast_to(row, (DK, row.shape[1])))


def local_terms(x_ref, rim_ref, w_ref, g_ref, upto):
    count = x_ref.shape[1]
    taps, mixed, sigs, acts = [], [], [], []
    for c in range(3):
        ext = jnp.concatenate([rim_ref[c].astype(F32), x_ref[c].astype(F32)], axis=0)
        rolled = [pltpu.roll(ext, KW - 1 - j, 0)[8:] if j < KW - 1 else ext[8:] for j in range(KW)]
        y = w_ref[c, 0:1] * rolled[0]
        for j in range(1, KW):
            y = y + w_ref[c, j : j + 1] * rolled[j]
        sig = 1.0 / (1.0 + jnp.exp(-y))
        taps.append(rolled)
        mixed.append(y)
        sigs.append(sig)
        acts.append(y * sig)
    rq = lax.rsqrt(jnp.sum(acts[0] * acts[0], axis=1, keepdims=True) + 1e-6)
    rk = lax.rsqrt(jnp.sum(acts[1] * acts[1], axis=1, keepdims=True) + 1e-6)
    q = acts[0] * rq * SCALE
    k = acts[1] * rk
    decays = dot(upto, g_ref[...], 1, 0)
    ends = [decays[b * BLOCK + BLOCK - 1 : (b + 1) * BLOCK] for b in range(count // BLOCK)]
    last = jnp.concatenate([jnp.broadcast_to(e, (BLOCK, DK)) for e in ends], axis=0)
    return taps, mixed, sigs, acts, rq, rk, q, k, decays, last, ends


def maps_kernel(
    resets_ref, x_ref, rim_ref, w_ref, g_ref, beta_ref, do_ref,
    x_out, w_out, u_out, pdo_out, mb_out, nb_out, gb_out, m_out, n_out, g_out,
):
    count = x_ref.shape[1]
    blocks = count // BLOCK
    group = x_out.shape[0]
    r, c, x = positions(count)
    inside = x < BLOCK
    upto_mask = inside & (r >= c)
    upto = upto_mask.astype(F32).astype(BF16)
    lower = r > c
    parts, ns, invs = [], [], []
    for i in range(group):
        lanes = pl.ds(i * DK, DK)
        taps, mixed, sigs, acts, rq, rk, q, k, decays, last, ends = local_terms(
            x_ref.at[:, :, lanes],
            rim_ref.at[:, :, lanes],
            w_ref.at[:, :, lanes],
            g_ref.at[:, lanes],
            upto,
        )
        grow = jnp.exp(decays)
        kp = k * grow
        km = split(k * jnp.exp(-decays))
        qb = split(q * grow)
        kf = split(k * jnp.exp(last - decays))
        beta = column(beta_ref[pl.ds(pl.program_id(0) * group + i, 1), :])
        wide = jnp.concatenate([beta] * (count // DK), axis=1)
        n = mm(split(kp), km, 1, 1) * wide
        right = jnp.concatenate([beta * acts[2], beta * kp], axis=1)
        parts.append((km, qb, kf, right, ends))
        ns.append(n)
        invs.append(jnp.where(r == c, 1.0, 0.0) - jnp.where(lower & (x < 2) & (x >= 1), n, 0.0))
    s = 2
    while s < BLOCK:
        here = lower & (x >= s) & (x < 2 * s)
        inv_s = [split(inv) for inv in invs]
        half = [mm(inv_s[i], split(jnp.where(here, ns[i], 0.0))) for i in range(group)]
        invs = [invs[i] - mm(split(half[i]), inv_s[i]) for i in range(group)]
        s *= 2
    er = lax.broadcasted_iota(jnp.int32, (DK, DK), 0) == lax.broadcasted_iota(jnp.int32, (DK, DK), 1)
    keeps = [1.0 - resets_ref[b].astype(F32) for b in range(blocks)]
    ms, nbs, gs = [], [], []
    for i in range(group):
        km, qb, kf, right, ends = parts[i]
        lanes = pl.ds(i * DK, DK)
        x_out[i] = invs[i]
        both = mm(split(invs[i]), split(right))
        u_out[:, lanes] = both[:, :DK]
        w_out[:, lanes] = both[:, DK:]
        do = (do_ref[:, lanes],)
        p = split(jnp.where(upto_mask, mm(qb, km, 1, 1), 0.0))
        pdo = mm(p, do, 0, 0)
        pdo_out[:, lanes] = pdo
        both_s = split(both)
        pdo_s = split(pdo)
        w_s = tuple(a[:, DK:] for a in both_s)
        m_list, n_list, g_list = [], [], []
        for b in range(blocks):
            nm = mm(rows_of(kf, b), rows_of(both_s, b), 0, 0)
            m = (jnp.where(er, jnp.exp(ends[b]), 0.0) - nm[:, DK:]) * keeps[b]
            g = mm(rows_of(qb, b), rows_of(do, b), 0, 0) - mm(
                rows_of(w_s, b), rows_of(pdo_s, b), 0, 0
            )
            g = g * keeps[b]
            mb_out[i, b] = m
            nb_out[i, b] = nm[:, :DK]
            gb_out[i, b] = g
            m_list.append((m, split(m)))
            n_list.append(nm[:, :DK])
            g_list.append(g)
        ms.append(m_list)
        nbs.append(n_list)
        gs.append(g_list)
    accs = [jnp.concatenate([ms[i][0][0], nbs[i][0]], axis=1) for i in range(group)]
    grads = [gs[i][-1] for i in range(group)]
    for b in range(1, blocks):
        back = blocks - 1 - b
        for i in range(group):
            acc = mm(ms[i][b][1], split(accs[i]))
            accs[i] = jnp.concatenate([acc[:, :DK], acc[:, DK:] + nbs[i][b]], axis=1)
            grads[i] = mm(ms[i][back][1], split(grads[i]), 0, 0) + gs[i][back]
    for i in range(group):
        m_out[i] = accs[i][:, :DK]
        n_out[i] = accs[i][:, DK:]
        g_out[i] = grads[i]


def grads_kernel(
    resets_ref, x_ref, rim_ref, w_ref, g_ref, beta_ref, do_ref,
    inv_ref, wm_ref, u_ref, pdo_ref, mb_ref, nb_ref, gb_ref, s_ref, ds_ref,
    dx_out, dg_out, db_out, dw_out, edge_out,
):
    count = x_ref.shape[1]
    blocks = count // BLOCK
    r, c, x = positions(count)
    inside = x < BLOCK
    upto_mask = inside & (r >= c)
    upto = upto_mask.astype(F32).astype(BF16)
    taps, mixed, sigs, acts, rq, rk, q, k, decays, last, ends = local_terms(
        x_ref, rim_ref, w_ref, g_ref, upto
    )
    v = acts[2]
    grow = jnp.exp(decays)
    shrink = jnp.exp(-decays)
    tail = jnp.exp(last - decays)
    kp, km, qb, kf = k * grow, k * shrink, q * grow, k * tail
    kp_s, km_s, qb_s, kf_s = split(kp), split(km), split(qb), split(kf)
    beta = column(beta_ref[pl.ds(pl.program_id(0), 1), :])
    do = do_ref[...]

    ms = [split(mb_ref[0, b]) for b in range(blocks)]
    states = []
    now = s_ref[0]
    for b in range(blocks):
        states.append(now * (1.0 - resets_ref[b].astype(F32)))
        if b < blocks - 1:
            now = mm(ms[b], split(now)) + nb_ref[0, b]
    states_s = [split(a) for a in states]
    after = [None] * blocks
    after[-1] = ds_ref[0]
    for b in range(blocks - 1, 0, -1):
        after[b - 1] = mm(ms[b], split(after[b]), 0, 0) + gb_ref[0, b]
    after_s = [split(a) for a in after]

    w_s = split(wm_ref[...])
    u = u_ref[...] - jnp.concatenate([mm(rows_of(w_s, b), states_s[b]) for b in range(blocks)], axis=0)
    u_s = split(u)
    du = pdo_ref[...] + jnp.concatenate([mm(rows_of(kf_s, b), after_s[b]) for b in range(blocks)], axis=0)
    drv = mm(split(inv_ref[0]), split(du), 0, 0)
    drv_s = split(drv)
    do_s = (do,)
    dp_s = split(jnp.where(upto_mask, mm(do_s, u_s, 1, 1), 0.0))
    dt = jnp.where(inside & (r > c), mm(drv_s, u_s, 1, 1), 0.0)
    dt_s = split(-dt)
    dq_state, drw, dkf, extra = [], [], [], []
    ones = (jnp.ones((8, DK), BF16),)
    for b in range(blocks):
        dq_state.append(mm(rows_of(do_s, b), states_s[b], 1, 1))
        drw.append(-mm(rows_of(drv_s, b), states_s[b], 1, 1))
        dkf.append(mm(rows_of(u_s, b), after_s[b], 1, 1))
        extra.append(mm(ones, split(states[b] * after[b]), 1, 1)[0:1] * jnp.exp(ends[b]))
    dqb = jnp.concatenate(dq_state, axis=0) + mm(dp_s, km_s)
    inner = jnp.concatenate(drw, axis=0) + mm(dt_s, km_s)
    dkf = jnp.concatenate(dkf, axis=0)
    dkp = beta * inner
    wide = jnp.concatenate([beta] * (count // DK), axis=1)
    da_s = split(-dt * wide)
    dkm = mm(dp_s, qb_s, 0, 0) + mm(da_s, kp_s, 0, 0)
    dbeta = jnp.sum(drv * v + kp * inner, axis=1, keepdims=True)
    db_out[pl.ds(pl.program_id(0), 1), :] = jnp.transpose(jnp.broadcast_to(dbeta, (count, DK)))[0:1]

    through = dkf * kf
    dd = dkp * kp - dkm * km - through + dqb * qb
    dg = mm((upto,), split(dd), 0, 0)
    whole = []
    for b in range(blocks):
        total = jnp.sum(through[b * BLOCK : (b + 1) * BLOCK], axis=0, keepdims=True) + extra[b]
        whole.append(jnp.broadcast_to(total, (BLOCK, DK)))
    dg_out[...] = (dg + jnp.concatenate(whole, axis=0)).astype(BF16)

    dq = dqb * grow
    dk = dkp * grow + dkm * shrink + dkf * tail
    dv = beta * drv
    da_q = SCALE * rq * dq - acts[0] * (rq * rq) * jnp.sum(q * dq, axis=1, keepdims=True)
    da_k = rk * dk - acts[1] * (rk * rk) * jnp.sum(k * dk, axis=1, keepdims=True)
    zeros = jnp.zeros((8, DK), F32)
    for ch, da in enumerate((da_q, da_k, dv)):
        dy = da * sigs[ch] * (1.0 + mixed[ch] * (1.0 - sigs[ch]))
        ext = jnp.concatenate([zeros, dy], axis=0)
        full = w_ref[ch, KW - 1 : KW] * ext
        for j in range(KW - 1):
            full = full + w_ref[ch, j : j + 1] * pltpu.roll(ext, count + 8 - (KW - 1 - j), 0)
        dx_out[ch] = full[8:].astype(BF16)
        edge_out[ch, 0:8] = full[0:8]
        edge_out[ch, 8:16] = full[count : count + 8]
        dw_out[ch] = jnp.concatenate(
            [jnp.sum(dy * taps[ch][j], axis=0, keepdims=True) for j in range(KW)], axis=0
        )


def chain_kernel(
    m_ref, n_ref, g_ref, state_out, grad_out,
    state, grad, send_f, send_b, f_sent, f_got, b_sent, b_got,
):
    heads = m_ref.shape[0]
    place = lax.axis_index("seq")
    count = lax.axis_size("seq")
    has_next = place < count - 1
    has_prev = place > 0
    after = {"seq": jnp.minimum(place + 1, count - 1)}
    before = {"seq": jnp.maximum(place - 1, 0)}
    mesh_ids = pl.DeviceIdType.MESH

    def forward(h, to):
        return pltpu.make_async_remote_copy(
            send_f.at[h], state.at[h], f_sent.at[h], f_got.at[h], to, mesh_ids
        )

    def backward(h, to):
        return pltpu.make_async_remote_copy(
            send_b.at[h], grad.at[h], b_sent.at[h], b_got.at[h], to, mesh_ids
        )

    barrier = pltpu.get_barrier_semaphore()

    @pl.when(has_next)
    def _():
        pl.semaphore_signal(barrier, inc=1, device_id=after, device_id_type=mesh_ids)

    @pl.when(has_prev)
    def _():
        pl.semaphore_signal(barrier, inc=1, device_id=before, device_id_type=mesh_ids)

    pl.semaphore_wait(barrier, has_next.astype(jnp.int32) + has_prev.astype(jnp.int32))

    @pl.when(place == 0)
    def _():
        state[...] = jnp.zeros_like(state)

    @pl.when(place == count - 1)
    def _():
        grad[...] = jnp.zeros_like(grad)

    def turn(t, carry):
        hf = t - place
        hb = t - (count - 1 - place)

        @pl.when((hf >= 0) & (hf < heads))
        def _():
            @pl.when(has_prev)
            def _():
                forward(hf, before).wait_recv()

            @pl.when(has_next)
            def _():
                send_f[hf] = mm(split(m_ref[hf]), split(state[hf])) + n_ref[hf]
                forward(hf, after).start()

        @pl.when((hb >= 0) & (hb < heads))
        def _():
            @pl.when(has_next)
            def _():
                backward(hb, after).wait_recv()

            @pl.when(has_prev)
            def _():
                send_b[hb] = mm(split(m_ref[hb]), split(grad[hb]), 0, 0) + g_ref[hb]
                backward(hb, before).start()

        return carry

    lax.fori_loop(0, heads + count - 1, turn, 0)

    def finish(h, carry):
        @pl.when(has_next)
        def _():
            forward(h, after).wait_send()

        @pl.when(has_prev)
        def _():
            backward(h, before).wait_send()

        return carry

    lax.fori_loop(0, heads, finish, 0)
    state_out[...] = state[...]
    grad_out[...] = grad[...]


def on_device(conv_inputs, conv_weight, gate_logs, beta_rates, state_resets, out_grad):
    count, channels = gate_logs.shape
    heads = beta_rates.shape[0]
    blocks = state_resets.shape[0]
    x3 = jnp.transpose(conv_inputs, (1, 0, 2))
    w3 = jnp.transpose(conv_weight, (1, 0, 2))
    rim = shifted(x3[:, count - 8 :], "seq", 1)

    smem = pl.BlockSpec(memory_space=pltpu.SMEM)
    tri = lambda n: pl.BlockSpec((3, n, DK), lambda h: (0, 0, h))
    rows = pl.BlockSpec((count, DK), lambda h: (0, h))
    whole = pl.BlockSpec((heads, count), lambda h: (0, 0))
    square = pl.BlockSpec((1, count, count), lambda h: (h, 0, 0))
    per_block = pl.BlockSpec((1, blocks, DK, DK), lambda h: (h, 0, 0, 0))
    per_head = pl.BlockSpec((1, DK, DK), lambda h: (h, 0, 0))
    common_specs = [smem, tri(count), tri(8), tri(KW), rows, whole, rows]
    common = (state_resets, x3, rim, w3, gate_logs, beta_rates, out_grad)
    shape = jax.ShapeDtypeStruct
    params = pltpu.CompilerParams(
        dimension_semantics=("arbitrary",), vmem_limit_bytes=48 * 1024 * 1024
    )
    rows_f32 = shape((count, channels), F32)
    blocks_f32 = shape((heads, blocks, DK, DK), F32)
    head_f32 = shape((heads, DK, DK), F32)
    group = 4 if heads % 4 == 0 else 2 if heads % 2 == 0 else 1
    tri_g = lambda n: pl.BlockSpec((3, n, group * DK), lambda h: (0, 0, h))
    rows_g = pl.BlockSpec((count, group * DK), lambda h: (0, h))
    square_g = pl.BlockSpec((group, count, count), lambda h: (h, 0, 0))
    per_block_g = pl.BlockSpec((group, blocks, DK, DK), lambda h: (h, 0, 0, 0))
    per_head_g = pl.BlockSpec((group, DK, DK), lambda h: (h, 0, 0))
    inv, w, u, pdo, mb, nb, gb, m, n, g = pl.pallas_call(
        maps_kernel,
        grid=(heads // group,),
        in_specs=[smem, tri_g(count), tri_g(8), tri_g(KW), rows_g, whole, rows_g],
        out_specs=[square_g, rows_g, rows_g, rows_g] + [per_block_g] * 3 + [per_head_g] * 3,
        out_shape=[shape((heads, count, count), F32), rows_f32, rows_f32, rows_f32]
        + [blocks_f32] * 3
        + [head_f32] * 3,
        compiler_params=params,
        name="maps",
    )(*common)

    vmem = pl.BlockSpec(memory_space=pltpu.VMEM)
    held = pltpu.VMEM((heads, DK, DK), F32)
    flags = pltpu.SemaphoreType.DMA((heads,))
    state, grad = pl.pallas_call(
        chain_kernel,
        in_specs=[vmem] * 3,
        out_specs=[vmem] * 2,
        out_shape=[head_f32] * 2,
        scratch_shapes=[held] * 4 + [flags] * 4,
        compiler_params=pltpu.CompilerParams(
            collective_id=0, has_side_effects=True, vmem_limit_bytes=32 * 1024 * 1024
        ),
        name="chain",
    )(m, n, g)

    dx, dg, db, dw, edge = pl.pallas_call(
        grads_kernel,
        grid=(heads,),
        in_specs=common_specs + [square, rows, rows, rows] + [per_block] * 3 + [per_head] * 2,
        out_specs=[tri(count), rows, whole, tri(KW), tri(16)],
        out_shape=[
            shape(x3.shape, BF16),
            shape((count, channels), BF16),
            shape((heads, count), F32),
            shape(w3.shape, F32),
            shape((3, 16, channels), F32),
        ],
        compiler_params=params,
        name="grads",
    )(*common, inv, w, u, pdo, mb, nb, gb, state, grad)
    spill = shifted(edge[:, :8], "seq", -1)
    dx = dx.at[:, count - 8 :].set((edge[:, 8:] + spill).astype(BF16))
    return (
        jnp.transpose(dx, (1, 0, 2)),
        dg,
        db,
        jnp.transpose(summed(dw, "seq"), (1, 0, 2)),
    )


def solution(mesh):
    in_specs = (
        P(("rep", "seq"), None, ("head", "sub")),
        P(None, None, ("head", "sub")),
        P(("rep", "seq"), ("head", "sub")),
        P(("head", "sub"), ("rep", "seq")),
        P(("rep", "seq")),
        P(("rep", "seq"), ("head", "sub")),
    )
    out_specs = (
        P(("rep", "seq"), None, ("head", "sub")),
        P(("rep", "seq"), ("head", "sub")),
        P(("head", "sub"), ("rep", "seq")),
        P("rep", None, ("head", "sub")),
    )
    return jax.shard_map(
        on_device, mesh=mesh, in_specs=in_specs, out_specs=out_specs, check_vma=False
    )
```
